256 devices in a mesh: dp: 16 (over z, core), seq: 16 (over y, x).
Axes of the slice: x: 4, y: 4, z: 8, core: 2. Of those that a mesh axis runs over, the one named last changes fastest.
Arguments:
- queries: bfloat16 [16, 4096, 2240], P('dp', 'seq'), may hold values from -6 to 6
- keys: bfloat16 [16, 4096, 2240], P('dp', 'seq'), may hold values from -1.5 to 1.5
- values: bfloat16 [16, 4096, 2240], P('dp', 'seq'), may hold values from -7 to 7
- cotangent: bfloat16 [16, 4096, 2240], P('dp', 'seq'), may hold values from -6 to 6
- conv_weight: float32 [2, 2240], replicated, may hold values from -3 to 3
Outputs:
- mixed: bfloat16 [16, 4096, 2240], P('dp', 'seq')
- grad_queries: bfloat16 [16, 4096, 2240], P('dp', 'seq')
- grad_keys: bfloat16 [16, 4096, 2240], P('dp', 'seq')
- grad_values: bfloat16 [16, 4096, 2240], P('dp', 'seq')
- conv_grad: float32 [2, 2240], replicated
The draws below stay inside these ranges and needn't reach their ends.
All inputs are finite; a program needn't handle non-finite values.
Results may differ from the reference program's by a relative error of at most 0.0047.
Values may be sent and summed in bfloat16 or wider, within the bound.
No kernel may reach another device: no remote copies, remote signals or barrier semaphores. Data moves between devices by JAX's collectives and lax.ppermute only.
A program may use at most 128 MiB of HBM per device.

```python
from functools import partial
import jax
import jax.numpy as jnp
from jax import lax

HEADS = 20
HEAD_DIM = 112
FRAME = 128
HE = 2240
LEN = 4096
CLIPS = 16


def draw_values(key, part):
    key = jax.random.fold_in(key, 7)
    frame_key, token_key = jax.random.split(key)
    frame_count = LEN // FRAME
    common = jax.random.normal(frame_key, (CLIPS, frame_count, 1, HE), jnp.float32)
    noise = jax.random.normal(token_key, (CLIPS, frame_count, FRAME, HE), jnp.float32)
    joined = jnp.clip(common + noise, -7.0, 7.0)
    return joined.reshape(CLIPS, LEN, HE).astype(jnp.bfloat16)


def block_scale(key, dims, pieces, smallest, top_value):
    def one(position, shards_of):
        draws = jax.random.uniform(jax.random.fold_in(jax.random.fold_in(key, 6), position), (shards_of,), jnp.float32, smallest / len(pieces), top_value / len(pieces))
        return jnp.repeat(jnp.exp(draws), dims[position] // shards_of).reshape((-1,) + (1,) * (len(dims) - position - 1))

    factor_of = one(*pieces[0])
    for cut in pieces[1:]:
        factor_of = factor_of * one(*cut)
    return factor_of


def centred(rng, shape, spread, bound, cuts=(), dtype=jnp.bfloat16):
    loudness = block_scale(rng, shape, cuts, -0.22, 0.18) if cuts else 1.0
    values = jax.random.normal(rng, shape, jnp.float32) * spread * loudness
    return jnp.minimum(jnp.maximum(values, -bound), bound).astype(dtype)


def setup_inputs(seed: int = 0) -> dict:
    key_of = jax.random.split(jax.random.key(seed), 6)
    return {
        "queries": centred(key_of[0], (CLIPS, LEN, HE), 1.0, 6.0, ((0, 16), (1, 16))),
        "keys": centred(key_of[1], (CLIPS, LEN, HE), 0.25, 1.5, ((0, 16), (1, 16))),
        "values": draw_values(jax.random.fold_in(key_of[5], 71), 0),
        "cotangent": centred(key_of[3], (CLIPS, LEN, HE), 1.0, 6.0, ((0, 16), (1, 16))),
        "conv_weight": centred(key_of[4], (2, HE), 0.5, 3.0, (), jnp.float32),
    }


denom_eps = 1e-6
loss_scale = 16.0


def suffix_sum(blocks):
    return jnp.flip(jnp.cumsum(jnp.flip(blocks, 0), 0), 0)


def clip_pass(inputs, conv_weight):
    queries, keys, values, cotangent = inputs
    frame_count = LEN // FRAME
    frame_shape = (frame_count, FRAME, HEADS, HEAD_DIM)
    highest = lax.Precision.HIGHEST
    q_feat = jnp.maximum(queries, 0).reshape(frame_shape).astype(jnp.float32)
    k_feat = jnp.maximum(keys, 0).reshape(frame_shape).astype(jnp.float32)
    v_wide = values.reshape(frame_shape).astype(jnp.float32)
    frame_kv = jnp.einsum('fthe,fthd->fhed', k_feat, v_wide, precision=highest)
    kv_state = jnp.cumsum(frame_kv, axis=0)
    key_sum = jnp.cumsum(jnp.sum(k_feat, axis=1), axis=0)
    numerator = jnp.einsum('fthe,fhed->fthd', q_feat, kv_state, precision=highest)
    denominator = jnp.einsum('fthe,fhe->fth', q_feat, key_sum, precision=highest) + denom_eps
    attended = (numerator / denominator[..., None]).astype(jnp.bfloat16).reshape(LEN, HE)
    wide_out = attended.astype(jnp.float32)
    one_back = jnp.pad(wide_out, ((FRAME, 0), (0, 0)))[:LEN]
    two_back = jnp.pad(wide_out, ((2 * FRAME, 0), (0, 0)))[:LEN]
    mixed = (wide_out + conv_weight[0] * one_back + conv_weight[1] * two_back).astype(jnp.bfloat16)
    cot_wide = cotangent.astype(jnp.float32)
    one_ahead = jnp.pad(cot_wide, ((0, FRAME), (0, 0)))[FRAME:]
    two_ahead = jnp.pad(cot_wide, ((0, 2 * FRAME), (0, 0)))[2 * FRAME:]
    grad_out = loss_scale * (cot_wide + conv_weight[0] * one_ahead + conv_weight[1] * two_ahead)
    conv_part = jnp.stack([jnp.sum(one_back * cot_wide, 0), jnp.sum(two_back * cot_wide, 0)])
    grad_frames = grad_out.reshape(frame_shape)
    grad_num = grad_frames / denominator[..., None]
    grad_den = -jnp.sum(grad_frames * numerator, -1) / (denominator * denominator)
    grad_state = suffix_sum(jnp.einsum('fthe,fthd->fhed', q_feat, grad_num, precision=highest))
    grad_keysum = suffix_sum(jnp.einsum('fth,fthe->fhe', grad_den, q_feat, precision=highest))
    grad_q = jnp.einsum('fthd,fhed->fthe', grad_num, kv_state, precision=highest) + grad_den[..., None] * key_sum[:, None]
    grad_v = jnp.einsum('fthe,fhed->fthd', k_feat, grad_state, precision=highest)
    grad_k = jnp.einsum('fthd,fhed->fthe', v_wide, grad_state, precision=highest) + grad_keysum[:, None]
    grad_queries = jnp.where(queries.reshape(frame_shape) > 0, grad_q, 0.0).astype(jnp.bfloat16).reshape(LEN, HE)
    grad_keys = jnp.where(keys.reshape(frame_shape) > 0, grad_k, 0.0).astype(jnp.bfloat16).reshape(LEN, HE)
    grad_values = grad_v.astype(jnp.bfloat16).reshape(LEN, HE)
    return mixed, grad_queries, grad_keys, grad_values, conv_part


def reference(queries, keys, values, cotangent, conv_weight):
    results = lax.map(partial(clip_pass, conv_weight=conv_weight), (queries, keys, values, cotangent))
    mixed, grad_queries, grad_keys, grad_values, conv_parts = results
    return mixed, grad_queries, grad_keys, grad_values, jnp.sum(conv_parts, 0) / CLIPS
```

```python
import functools

import jax
import jax.numpy as jnp
from jax import lax
from jax.experimental import pallas as pl
from jax.experimental.pallas import tpu as pltpu
from jax.sharding import PartitionSpec as P

HEADS = 20
HEAD_DIM = 112
FRAME = 128
LANES = 128
GROUP = 8
WIDTH = GROUP * HEAD_DIM
STEPS = -(-HEADS // GROUP)
LAST = HEADS - (STEPS - 1) * GROUP

denom_eps = 1e-06
loss_scale = 16.0
f32 = jnp.float32
bf16 = jnp.bfloat16


def lane_of(rows):
    return lax.broadcasted_iota(jnp.int32, (rows, LANES), 1)


def tile(ref, a, rows=slice(None)):
    return ref[rows, a * LANES : (a + 1) * LANES]


def take_head(ref, j, rows=slice(None)):
    if j == 0:
        return tile(ref, 0, rows)
    shift = (LANES - HEAD_DIM) * j
    if j == GROUP - 1:
        both = tile(ref, j - 1, rows)
    else:
        low, high = tile(ref, j - 1, rows), tile(ref, j, rows)
        both = jnp.where(lane_of(low.shape[0]) >= LANES - shift, low, high)
    return pltpu.roll(both, shift, 1)


def put_back(block, j):
    shift = (LANES - HEAD_DIM) * j
    return block if j == 0 else pltpu.roll(block, LANES - shift, 1)


def join_tiles(a, first, second):
    edge = HEAD_DIM - (LANES - HEAD_DIM) * a
    return jnp.where(lane_of(first.shape[0]) < edge, first, second)


def split(x):
    high = x.astype(bf16)
    return high, (x - high.astype(f32)).astype(bf16)


def dot(a, b, ca, cb):
    return lax.dot_general(a, b, (((ca,), (cb,)), ((), ())), preferred_element_type=f32)


def keep(x, fill=0.0):
    return jnp.where(lane_of(x.shape[0]) < HEAD_DIM, x, jnp.asarray(fill, x.dtype))


def with_one(x):
    lane = lane_of(x.shape[0])
    tail = jnp.where(lane == HEAD_DIM, 1.0, 0.0).astype(x.dtype)
    return jnp.where(lane < HEAD_DIM, x, tail)


def pad_rows(x):
    return jnp.concatenate([x, jnp.zeros((LANES - HEAD_DIM, x.shape[1]), x.dtype)], axis=0)


def each_head(work, flush):
    last = pl.program_id(0) == STEPS - 1

    @pl.when(jnp.logical_not(last))
    def _():
        flush([work(j) for j in range(GROUP)])

    @pl.when(last)
    def _():
        flush([work(j) for j in range(LAST)])


def write_tiles(ref, blocks, rows):
    n = len(blocks)
    for a in range(min(n, GROUP - 1)):
        second = blocks[a + 1] if a + 1 < n else blocks[a]
        ref[rows, a * LANES : (a + 1) * LANES] = join_tiles(a, blocks[a], second)


def state_kernel(k_ref, v_ref, tot_ref, first_ref):
    def work(j):
        k = jnp.maximum(take_head(k_ref, j), 0)
        v = with_one(take_head(v_ref, j))
        s0 = dot(k[:FRAME], v[:FRAME], 0, 0)[:HEAD_DIM]
        s1 = dot(k[FRAME:], v[FRAME:], 0, 0)[:HEAD_DIM]
        rows = slice(j * HEAD_DIM, (j + 1) * HEAD_DIM)
        first_ref[rows, :] = s0
        tot_ref[rows, :] = s0 + s1

    each_head(work, lambda _: None)


def scan_kernel(backward, x_ref, o_ref):
    n = x_ref.shape[0]
    order = range(n - 1, -1, -1) if backward else range(n)
    total = jnp.zeros(x_ref.shape[1:], f32)
    for i in order:
        o_ref[i] = total
        total = total + x_ref[i]


def middle_kernel(
    q_ref, cot_ref, next_ref, w_ref, prev_ref, tot_ref, first_ref,
    att_ref, gq_ref, gtot_ref, glast_ref, conv_ref, go_ref,
):
    frames = [slice(0, FRAME), slice(FRAME, 2 * FRAME)]
    for a in range(WIDTH // LANES):
        cols = slice(a * LANES, (a + 1) * LANES)
        c = [ref[r, cols].astype(f32) for ref in (cot_ref, next_ref) for r in frames]
        w0, w1 = w_ref[0:1, cols], w_ref[1:2, cols]
        for f in range(2):
            go_ref[frames[f], cols] = loss_scale * (c[f] + w0 * c[f + 1] + w1 * c[f + 2])

    def work(j):
        rows = slice(j * HEAD_DIM, (j + 1) * HEAD_DIM)
        q = keep(jnp.maximum(take_head(q_ref, j), 0))
        lane = lane_of(FRAME)
        atts, grads, gstates = [], [], []
        for f in range(2):
            own = (first_ref, tot_ref)[f]
            hi, lo = (pad_rows(x) for x in split(prev_ref[rows, :] + own[rows, :]))
            qf = q[frames[f]]
            num = dot(jnp.concatenate([qf, qf], 1), jnp.concatenate([hi, lo], 0), 1, 0)
            inv = 1.0 / (num[:, HEAD_DIM : HEAD_DIM + 1] + denom_eps)
            atts.append(put_back((num * inv).astype(bf16), j))
            gn = keep(take_head(go_ref, j, frames[f])) * inv
            gden = -inv * jnp.sum(gn * num, axis=1, keepdims=True)
            ghi, glo = split(jnp.where(lane == HEAD_DIM, gden, gn))
            gstates.append(
                dot(jnp.concatenate([qf, qf], 0), jnp.concatenate([ghi, glo], 0), 0, 0)[:HEAD_DIM]
            )
            gq = dot(
                jnp.concatenate([ghi, glo, ghi], 1), jnp.concatenate([hi, hi, lo], 1), 1, 1
            )
            gq = jnp.where(qf.astype(f32) > 0, gq, 0.0)
            grads.append(put_back(gq.astype(bf16), j))
        glast_ref[rows, :] = gstates[1]
        gtot_ref[rows, :] = gstates[0] + gstates[1]
        return atts, grads

    def flush(parts):
        for f in range(2):
            write_tiles(att_ref, [p[0][f] for p in parts], frames[f])
            write_tiles(gq_ref, [p[1][f] for p in parts], frames[f])

    each_head(work, flush)
    for a in range(WIDTH // LANES):
        cols = slice(a * LANES, (a + 1) * LANES)
        c = [ref[r, cols].astype(f32) for ref in (cot_ref, next_ref) for r in frames]
        att = [att_ref[r, cols].astype(f32) for r in frames]
        for i in range(2):
            conv_ref[i : i + 1, cols] = jnp.sum(
                att[0] * c[i + 1] + att[1] * c[i + 2], axis=0, keepdims=True
            )


def last_kernel(
    k_ref, v_ref, att_ref, back_ref, w_ref, next_ref, gtot_ref, glast_ref,
    mix_ref, gk_ref, gv_ref,
):
    frames = [slice(0, FRAME), slice(FRAME, 2 * FRAME)]

    def work(j):
        rows = slice(j * HEAD_DIM, (j + 1) * HEAD_DIM)
        k = keep(jnp.maximum(take_head(k_ref, j), 0))
        v = with_one(take_head(v_ref, j))
        gks, gvs = [], []
        for f in range(2):
            own = (gtot_ref, glast_ref)[f]
            hi, lo = (pad_rows(x) for x in split(next_ref[rows, :] + own[rows, :]))
            kf, vf = k[frames[f]], v[frames[f]]
            gv = dot(jnp.concatenate([kf, kf], 1), jnp.concatenate([hi, lo], 0), 1, 0)
            gk = dot(jnp.concatenate([vf, vf], 1), jnp.concatenate([hi, lo], 1), 1, 1)
            gk = jnp.where(kf.astype(f32) > 0, gk, 0.0)
            gvs.append(put_back(gv.astype(bf16), j))
            gks.append(put_back(gk.astype(bf16), j))
        return gks, gvs

    def flush(parts):
        for f in range(2):
            write_tiles(gk_ref, [p[0][f] for p in parts], frames[f])
            write_tiles(gv_ref, [p[1][f] for p in parts], frames[f])

    each_head(work, flush)
    for a in range(WIDTH // LANES):
        cols = slice(a * LANES, (a + 1) * LANES)
        c = [ref[r, cols].astype(f32) for ref in (back_ref, att_ref) for r in frames]
        w0, w1 = w_ref[0:1, cols], w_ref[1:2, cols]
        for f in range(2):
            mix_ref[frames[f], cols] = (c[f + 2] + w0 * c[f + 1] + w1 * c[f]).astype(bf16)


def call(kernel, name, outs, *args, scratch=(), cost=None):
    tok = pl.BlockSpec((2 * FRAME, WIDTH), lambda g: (0, g))
    state = pl.BlockSpec((WIDTH, LANES), lambda g: (g, 0))
    pair = pl.BlockSpec((2, WIDTH), lambda g: (0, g))

    def spec(x):
        return pair if x.shape[0] == 2 else (state if x.shape[1] == LANES else tok)

    return pl.pallas_call(
        kernel,
        grid=(STEPS,),
        in_specs=[spec(a) for a in args],
        out_specs=[spec(o) for o in outs],
        out_shape=outs,
        scratch_shapes=list(scratch),
        compiler_params=pltpu.CompilerParams(vmem_limit_bytes=40 * 2**20),
        name=name,
    )(*args)


def exclusive_sum(x, axis, backward):
    n = lax.axis_size(axis)
    pieces = x.reshape(n, x.shape[0] // n, LANES)
    pieces = lax.all_to_all(pieces, axis, 0, 0, tiled=True)
    sums = pl.pallas_call(
        functools.partial(scan_kernel, backward),
        out_shape=jax.ShapeDtypeStruct(pieces.shape, f32),
        compiler_params=pltpu.CompilerParams(vmem_limit_bytes=40 * 2**20),
        name="scan",
    )(pieces)
    return lax.all_to_all(sums, axis, 0, 0, tiled=True).reshape(x.shape)


def from_behind(block, axis, distance):
    devices = range(lax.axis_size(axis))
    route = [(i - distance, i) for i in devices if i - distance in devices]
    return lax.ppermute(block, axis, route)


def body(queries, keys, values, cotangent, conv_weight):
    clips, toks, width = queries.shape
    q, k, v, cot = (x.reshape(toks, width) for x in (queries, keys, values, cotangent))
    n = lax.axis_size("seq")
    unit = 16 * n
    rows = -(-HEADS * HEAD_DIM // unit) * unit
    state = jax.ShapeDtypeStruct((rows, LANES), f32)
    tokens = jax.ShapeDtypeStruct((toks, width), bf16)

    cot_next = from_behind(cot, "seq", -1)
    tot, first = call(state_kernel, "states", [state, state], k, v)
    prev = exclusive_sum(tot, "seq", False)
    att, gq, gtot, glast, conv = call(
        middle_kernel, "middle",
        [tokens, tokens, state, state, jax.ShapeDtypeStruct((2, width), f32)],
        q, cot, cot_next, conv_weight, prev, tot, first,
        scratch=[pltpu.VMEM((2 * FRAME, WIDTH), f32)],
    )
    back = from_behind(att, "seq", 1)
    conv = jnp.sum(lax.all_gather(conv, "seq"), 0)
    conv = jnp.sum(lax.all_gather(conv, "dp"), 0) / (clips * lax.axis_size("dp"))
    follow = exclusive_sum(gtot, "seq", True)
    mixed, gk, gv = call(
        last_kernel, "last", [tokens] * 3, k, v, att, back, conv_weight, follow, gtot, glast
    )
    return tuple(x.reshape(clips, toks, width) for x in (mixed, gq, gk, gv)) + (conv,)


def solution(mesh):
    blocks = P("dp", "seq", None)
    return jax.shard_map(
        body,
        mesh=mesh,
        in_specs=(blocks,) * 4 + (P(),),
        out_specs=(blocks,) * 4 + (P(),),
        check_vma=False,
    )
```

```python
import functools

import jax
import jax.numpy as jnp
from jax import lax
from jax.experimental import pallas as pl
from jax.experimental.pallas import tpu as pltpu
from jax.sharding import PartitionSpec as P

HEADS = 20
HEAD_DIM = 112
FRAME = 128
LANES = 128
HALF = HEADS // 2
HALF_ROWS = HALF * HEAD_DIM
PIECE = 16
TOLD = 48
WIRE = jnp.bfloat16
SCAN_STEPS = 1

denom_eps = 1e-06
loss_scale = 16.0
f32 = jnp.float32
bf16 = jnp.bfloat16

PARAMS = pltpu.CompilerParams(vmem_limit_bytes=56 * 2**20)
frames = [slice(0, FRAME), slice(FRAME, 2 * FRAME)]
units = [(j, f) for j in range(HALF) for f in range(2)]


def shape(*dims, dtype=f32):
    return jax.ShapeDtypeStruct(dims, dtype)


def split(x):
    high = x.astype(bf16)
    return high, (x - high.astype(f32)).astype(bf16)


def dot(a, b, ca, cb):
    return lax.dot_general(a, b, (((ca,), (cb,)), ((), ())), preferred_element_type=f32)


def cat(parts, axis):
    return jnp.concatenate(parts, axis=axis)


def first_of_pad(columns):
    return lax.broadcasted_iota(jnp.int32, (LANES - HEAD_DIM, columns), 0) == 0


def with_one(v):
    return cat([v, jnp.where(first_of_pad(v.shape[1]), 1.0, 0.0).astype(bf16)], 0)


def rows_of(j):
    return slice(j * HEAD_DIM, (j + 1) * HEAD_DIM)


def filtered(c, w_ref, rows):
    w0, w1 = w_ref[rows, 0:1], w_ref[rows, 1:2]
    return c[0] + w0 * c[1] + w1 * c[2]


def parts_of(rows, *refs):
    return [ref[rows, fr].astype(f32) for ref in refs for fr in frames]


def grid_of(rows):
    dims = (rows // PIECE, PIECE, LANES)
    return [lax.broadcasted_iota(jnp.int32, dims, d) for d in (2, 1)]


def slots():
    channel = lax.broadcasted_iota(jnp.int32, (LANES, LANES), 0)
    column = lax.broadcasted_iota(jnp.int32, (LANES, LANES), 1)
    hit = (channel < HEAD_DIM) & (column - (HEAD_DIM + 2) == channel // PIECE)
    return jnp.where(hit, 1.0, 0.0).astype(bf16)


def encode(x):
    lane, row = grid_of(x.shape[0])
    x3 = x.reshape(lane.shape)
    sums = jnp.sum(x3, axis=1, keepdims=True)
    mean = sums / (sums[:, :, HEAD_DIM : HEAD_DIM + 1] + 1e-30)
    mean = jnp.where(lane[:, :1] < HEAD_DIM, mean, 0.0).astype(bf16).astype(f32)
    key_sum = x3[:, :, HEAD_DIM : HEAD_DIM + 1]
    low = key_sum - key_sum.astype(bf16).astype(f32)
    y = jnp.where(lane == HEAD_DIM + 1, low, x3 - key_sum * mean)
    kept = jnp.where(lane % PIECE == row, mean, 0.0).reshape(x.shape).astype(bf16)
    return (y.reshape(x.shape) + dot(kept, slots(), 1, 0)).astype(WIRE)


def decode(y):
    lane, row = grid_of(y.shape[0])
    column = lax.broadcasted_iota(jnp.int32, (LANES, LANES), 1)
    pair = (column == HEAD_DIM) | (column == HEAD_DIM + 1)
    pair = jnp.where(pair, 1.0, 0.0).astype(bf16)
    both = dot(y, cat([slots(), pair], 0), 1, 1)
    key_sum = both[:, LANES:].reshape(lane.shape)
    mean = jnp.where(lane % PIECE == row, both[:, :LANES].reshape(lane.shape), 0.0)
    mean = jnp.sum(mean, axis=1, keepdims=True)
    x = y.astype(f32).reshape(lane.shape) + key_sum * mean
    x = jnp.where(lane < HEAD_DIM, x, jnp.where(lane == HEAD_DIM, key_sum, 0.0))
    return x.reshape(y.shape)


def encode_grad(x):
    lane = lax.broadcasted_iota(jnp.int32, x.shape, 1)
    low = pltpu.roll(x - x.astype(bf16).astype(f32), 1, 1)
    return jnp.where(lane == HEAD_DIM + 1, low, x).astype(WIRE)


def decode_grad(y):
    lane = lax.broadcasted_iota(jnp.int32, y.shape, 1)
    x = y.astype(f32)
    whole = x + pltpu.roll(x, LANES - 1, 1)
    return jnp.where(lane < HEAD_DIM, x, jnp.where(lane == HEAD_DIM, whole, 0.0))


def state_kernel(k_ref, v_ref, tot_ref, first_ref, send_ref):
    ks = [jnp.maximum(k_ref[rows_of(j), :], 0) for j in range(HALF)]
    vs = [with_one(v_ref[rows_of(j), :]) for j in range(HALF)]
    firsts = [dot(k[:, :FRAME], v[:, :FRAME], 1, 1) for k, v in zip(ks, vs)]
    seconds = [dot(k[:, FRAME:], v[:, FRAME:], 1, 1) for k, v in zip(ks, vs)]
    for j in range(HALF):
        tot = firsts[j] + seconds[j]
        first_ref[rows_of(j), :] = firsts[j]
        tot_ref[rows_of(j), :] = tot
        send_ref[rows_of(j), :] = encode(tot)


def scan_kernel(x_ref, o_ref):
    parts = [decode(x_ref[i]) for i in range(x_ref.shape[0])]
    totals = [jnp.zeros_like(parts[0])]
    for part in parts[:-1]:
        totals.append(totals[-1] + part)
    for i, total in enumerate([encode(total) for total in totals]):
        o_ref[i] = total


def scan_back_kernel(x_ref, o_ref, sum_ref):
    n, rows = o_ref.shape[:2]
    parts = [decode_grad(x_ref[i, :rows]) for i in range(n)]
    totals = [jnp.zeros_like(parts[0])]
    for part in parts[:0:-1]:
        totals.append(totals[-1] + part)
    for i, total in enumerate([encode_grad(total) for total in totals]):
        o_ref[n - 1 - i] = total
    sum_ref[...] = sum(x_ref[i, rows:].astype(f32) for i in range(n))


def numerators(qs, states):
    nums = {u: dot(cat(states[u], 0), cat([qs[u]] * 2, 0), 0, 0) for u in qs}
    invs = {u: 1.0 / (num[HEAD_DIM : HEAD_DIM + 1] + denom_eps) for u, num in nums.items()}
    return {u: num[:HEAD_DIM] for u, num in nums.items()}, invs


def gradients(go, num, inv):
    gn = go * inv
    gden = -inv * jnp.sum(gn * num, axis=0, keepdims=True)
    return split(cat([gn, jnp.where(first_of_pad(FRAME), gden, 0.0)], 0))


def middle_kernel(
    chunk, q_ref, behind_ref, cot_ref, ahead_ref, w_ref, prev_ref, tot_ref, first_ref,
    att0_ref, att1_ref, att_behind_ref, gtot_ref, glast_ref, send_ref, conv_ref,
):
    step = pl.program_id(0)
    stride = chunk + TOLD
    qs, states, cots, gos = {}, {}, {}, {}
    for j in range(HALF):
        rows = rows_of(j)
        q = jnp.maximum(q_ref[rows, :], 0)
        before = decode(prev_ref[rows, :])
        qs[j, -1] = jnp.maximum(behind_ref[rows, :], 0)
        states[j, -1] = split(before)
        for f in range(2):
            qs[j, f] = q[:, frames[f]]
            states[j, f] = split(before + (first_ref, tot_ref)[f][rows, :])
        w0, w1 = w_ref[rows, 0:1], w_ref[rows, 1:2]
        c0, c1 = parts_of(rows, cot_ref)
        c2 = ahead_ref[rows, :].astype(f32)
        cots[j] = c0, c1, c2
        gos[j, -1] = loss_scale * (w1 * c1)
        gos[j, 0] = loss_scale * (c0 + w0 * c1 + w1 * c2)
        gos[j, 1] = loss_scale * (c1 + w0 * c2)
    nums, invs = numerators(qs, states)
    atts = {u: (nums[u] * invs[u]).astype(bf16) for u in qs}
    grads = {u: gradients(gos[u], nums[u], invs[u]) for u in qs}
    gstates = {u: dot(cat([qs[u]] * 2, 1), cat(grads[u], 1), 1, 1) for u in qs}
    for j in range(HALF):
        rows = rows_of(j)
        own = gstates[j, 0] + gstates[j, 1]
        glast_ref[rows, :] = gstates[j, 1]
        gtot_ref[rows, :] = own
        wire = encode_grad(own + gstates[j, -1])
        for at in range(rows.start, rows.stop, PIECE):
            to = step * (send_ref.shape[0] // 2) + at // chunk * stride + at % chunk
            piece = wire[at - rows.start : at - rows.start + PIECE]
            send_ref[pl.ds(pl.multiple_of(to, PIECE), PIECE), :] = piece
        att_behind_ref[rows, :], att0_ref[rows, :], att1_ref[rows, :] = (
            atts[j, f] for f in (-1, 0, 1)
        )
        wide = [atts[j, f].astype(f32) for f in (-1, 0)]
        c0, c1, c2 = cots[j]
        for i, part in enumerate([wide[0] * c0 + wide[1] * c1, wide[0] * c1 + wide[1] * c2]):
            line = jnp.sum(part.T, axis=0, keepdims=True)
            line = cat([line, jnp.zeros((1, LANES - HEAD_DIM), f32)], 1)
            conv_ref[pl.ds(i * HEADS + step * HALF + j, 1), :] = line

    @pl.when(step == 1)
    def _():
        conv_ref[2 * HEADS :, :] = jnp.zeros((TOLD - 2 * HEADS, LANES), f32)
        conv = conv_ref[...].astype(send_ref.dtype)
        for i in range(send_ref.shape[0] // stride):
            send_ref[i * stride + chunk : (i + 1) * stride, :] = conv


def queries_kernel(
    q_ref, cot_ref, ahead_ref, ahead2_ref, w_ref, prev_ref, tot_ref, first_ref, gq_ref
):
    qs, states, gos = {}, {}, {}
    for j in range(HALF):
        rows = rows_of(j)
        q = jnp.maximum(q_ref[rows, :], 0)
        before = decode(prev_ref[rows, :])
        c = parts_of(rows, cot_ref) + [r[rows, :].astype(f32) for r in (ahead_ref, ahead2_ref)]
        for f in range(2):
            qs[j, f] = q[:, frames[f]]
            states[j, f] = split(before + (first_ref, tot_ref)[f][rows, :])
            gos[j, f] = loss_scale * filtered(c[f : f + 3], w_ref, rows)
    nums, invs = numerators(qs, states)
    for j, f in qs:
        u = j, f
        (hi, lo), (ghi, glo) = states[u], gradients(gos[u], nums[u], invs[u])
        gq = dot(cat([hi, hi, lo], 1), cat([ghi, glo, ghi], 0), 1, 0)
        gq = jnp.where(qs[u].astype(f32) > 0, gq, 0.0)
        gq_ref[rows_of(j), frames[f]] = gq.astype(bf16)


def mixed_kernel(att0_ref, att1_ref, behind_ref, behind2_ref, w_ref, mix_ref):
    for j in range(HALF):
        rows = rows_of(j)
        c = [r[rows, :].astype(f32) for r in (behind2_ref, behind_ref, att0_ref, att1_ref)]
        for f in range(2):
            mix_ref[rows, frames[f]] = filtered(c[f : f + 3][::-1], w_ref, rows).astype(bf16)


def last_kernel(k_ref, v_ref, follow_ref, gtot_ref, glast_ref, gk_ref, gv_ref):
    ks, vs, states = {}, {}, {}
    for j in range(HALF):
        rows = rows_of(j)
        k = jnp.maximum(k_ref[rows, :], 0)
        v = with_one(v_ref[rows, :])
        behind = decode_grad(follow_ref[rows, :])
        for f in range(2):
            ks[j, f], vs[j, f] = k[:, frames[f]], v[:, frames[f]]
            states[j, f] = split(behind + (gtot_ref, glast_ref)[f][rows, :])
    gvs = {u: dot(cat(states[u], 0), cat([ks[u]] * 2, 0), 0, 0) for u in units}
    gks = {u: dot(cat(states[u], 1), cat([vs[u]] * 2, 0), 1, 0) for u in units}
    for j, f in units:
        rows = rows_of(j)
        gv_ref[rows, frames[f]] = gvs[j, f][:HEAD_DIM].astype(bf16)
        gk = jnp.where(ks[j, f].astype(f32) > 0, gks[j, f], 0.0)
        gk_ref[rows, frames[f]] = gk.astype(bf16)


def call(kernel, name, outs, *args, whole=()):
    def spec(x):
        if any(x is w for w in whole):
            return pl.BlockSpec(x.shape, lambda g: (0, 0))
        return pl.BlockSpec((x.shape[0] // 2, x.shape[1]), lambda g: (g, 0))

    return pl.pallas_call(
        kernel,
        grid=(2,),
        in_specs=[spec(a) for a in args],
        out_specs=[spec(o) for o in outs],
        out_shape=outs,
        compiler_params=PARAMS,
        name=name,
    )(*args)


def scan(x):
    n, rows = x.shape[:2]
    block = pl.BlockSpec((n, rows // SCAN_STEPS, LANES), lambda g: (0, g, 0))
    return pl.pallas_call(
        scan_kernel, grid=(SCAN_STEPS,), in_specs=[block], out_specs=block,
        out_shape=shape(*x.shape, dtype=WIRE), compiler_params=PARAMS, name="scan",
    )(x)


def scan_back(x):
    n, rows = x.shape[:2]
    return pl.pallas_call(
        scan_back_kernel,
        out_shape=(shape(n, rows - TOLD, LANES, dtype=WIRE), shape(TOLD, LANES)),
        compiler_params=PARAMS,
        name="scan_back",
    )(x)


def exchange(x, axis):
    return lax.all_to_all(x, axis, 0, 0, tiled=True)


def from_behind(block, axis, distance):
    devices = range(lax.axis_size(axis))
    route = [(i - distance, i) for i in devices if i - distance in devices]
    return lax.ppermute(block, axis, route)


def total_over(x, axis):
    n = lax.axis_size(axis)
    bit = 1
    while bit < n:
        masks = [bit] if 2 * bit == n else [bit, 2 * bit, 3 * bit]
        x = x + sum(lax.ppermute(x, axis, [(i, i ^ m) for i in range(n)]) for m in masks)
        bit *= 4
    return x


def body(queries, keys, values, cotangent, conv_weight):
    clips, toks, width = queries.shape
    q, k, v, cot = (x.reshape(toks, width).T for x in (queries, keys, values, cotangent))
    weight = conv_weight.T
    n = lax.axis_size("seq")
    chunk = -(-HALF_ROWS // (PIECE * (n // 2))) * PIECE
    state = shape(chunk * n, LANES)
    sent = shape(*state.shape, dtype=WIRE)
    tokens = shape(width, toks, dtype=bf16)

    half_tokens = shape(width, FRAME, dtype=bf16)

    behind = from_behind(q[:, FRAME:], "seq", 1)
    ahead = from_behind(cot[:, :FRAME], "seq", -1)
    tot, first, send = call(state_kernel, "states", [state, state, sent], k, v)
    got = exchange(send.reshape(n, chunk, LANES), "seq")
    prev = exchange(scan(got), "seq").reshape(state.shape)
    ahead2, prev = lax.optimization_barrier((cot[:, FRAME:], prev))
    ahead2 = from_behind(ahead2, "seq", -1)
    send, conv = shape(n * (chunk + TOLD), LANES, dtype=WIRE), shape(TOLD, LANES)
    att0, att1, att_behind, gtot, glast, send, _ = call(
        functools.partial(middle_kernel, chunk), "middle",
        [half_tokens, half_tokens, half_tokens, state, state, send, conv],
        q, behind, cot, ahead, weight, prev, tot, first, whole=[send, conv],
    )
    got = exchange(send.reshape(n, chunk + TOLD, LANES), "seq")
    att_behind2 = from_behind(att0, "seq", 1)
    follow, conv = scan_back(got)
    follow = exchange(follow, "seq").reshape(state.shape)
    (gq,) = call(
        queries_kernel, "queries", [tokens], q, cot, ahead, ahead2, weight, prev, tot, first
    )
    (mixed,) = call(
        mixed_kernel, "mixed", [tokens], att0, att1, att_behind, att_behind2, weight
    )
    conv = total_over(lax.optimization_barrier((conv, mixed))[0], "dp")
    conv = conv[: 2 * HEADS].reshape(2, HEADS, LANES)[:, :, :HEAD_DIM].reshape(2, width)
    conv = conv / (clips * lax.axis_size("dp"))
    gk, gv = call(last_kernel, "last", [tokens] * 2, k, v, follow, gtot, glast)
    return tuple(x.T.reshape(clips, toks, width) for x in (mixed, gq, gk, gv)) + (conv,)


def solution(mesh):
    blocks = P("dp", "seq", None)
    return jax.shard_map(
        body,
        mesh=mesh,
        in_specs=(blocks,) * 4 + (P(),),
        out_specs=(blocks,) * 4 + (P(),),
        check_vma=False,
    )
```

```python
import functools

import jax
import jax.numpy as jnp
from jax import lax
from jax.experimental import pallas as pl
from jax.experimental.pallas import tpu as pltpu
from jax.sharding import PartitionSpec as P

HEADS = 20
HEAD_DIM = 112
FRAME = 128
LANES = 128
HALF = HEADS // 2
HALF_ROWS = HALF * HEAD_DIM
PIECE = 16
TOLD = 48
WIRE = jnp.bfloat16

denom_eps = 1e-06
loss_scale = 16.0
f32 = jnp.float32
bf16 = jnp.bfloat16

PARAMS = pltpu.CompilerParams(vmem_limit_bytes=56 * 2**20)
frames = [slice(0, FRAME), slice(FRAME, 2 * FRAME)]
units = [(j, f) for j in range(HALF) for f in range(2)]


def shape(*dims, dtype=f32):
    return jax.ShapeDtypeStruct(dims, dtype)


def split(x):
    high = x.astype(bf16)
    return high, (x - high.astype(f32)).astype(bf16)


def dot(a, b, ca, cb):
    return lax.dot_general(a, b, (((ca,), (cb,)), ((), ())), preferred_element_type=f32)


def cat(parts, axis):
    return jnp.concatenate(parts, axis=axis)


def first_of_pad(columns):
    return lax.broadcasted_iota(jnp.int32, (LANES - HEAD_DIM, columns), 0) == 0


def with_one(v):
    return cat([v, jnp.where(first_of_pad(v.shape[1]), 1.0, 0.0).astype(bf16)], 0)


def rows_of(j):
    return slice(j * HEAD_DIM, (j + 1) * HEAD_DIM)


def filtered(c, w_ref, rows):
    w0, w1 = w_ref[rows, 0:1], w_ref[rows, 1:2]
    return c[0] + w0 * c[1] + w1 * c[2]


def parts_of(rows, *refs):
    return [ref[rows, fr].astype(f32) for ref in refs for fr in frames]


def grid_of(rows):
    dims = (rows // PIECE, PIECE, LANES)
    return [lax.broadcasted_iota(jnp.int32, dims, d) for d in (2, 1)]


def slots():
    channel = lax.broadcasted_iota(jnp.int32, (LANES, LANES), 0)
    column = lax.broadcasted_iota(jnp.int32, (LANES, LANES), 1)
    hit = (channel < HEAD_DIM) & (column - (HEAD_DIM + 2) == channel // PIECE)
    return jnp.where(hit, 1.0, 0.0).astype(bf16)


def encode(x):
    lane, row = grid_of(x.shape[0])
    x3 = x.reshape(lane.shape)
    sums = jnp.sum(x3, axis=1, keepdims=True)
    mean = sums / (sums[:, :, HEAD_DIM : HEAD_DIM + 1] + 1e-30)
    mean = jnp.where(lane[:, :1] < HEAD_DIM, mean, 0.0).astype(bf16).astype(f32)
    key_sum = x3[:, :, HEAD_DIM : HEAD_DIM + 1]
    low = key_sum - key_sum.astype(bf16).astype(f32)
    y = jnp.where(lane == HEAD_DIM + 1, low, x3 - key_sum * mean)
    kept = jnp.where(lane % PIECE == row, mean, 0.0).reshape(x.shape).astype(bf16)
    return (y.reshape(x.shape) + dot(kept, slots(), 1, 0)).astype(WIRE)


def decode(y):
    lane, row = grid_of(y.shape[0])
    column = lax.broadcasted_iota(jnp.int32, (LANES, LANES), 1)
    pair = (column == HEAD_DIM) | (column == HEAD_DIM + 1)
    pair = jnp.where(pair, 1.0, 0.0).astype(bf16)
    both = dot(y, cat([slots(), pair], 0), 1, 1)
    key_sum = both[:, LANES:].reshape(lane.shape)
    mean = jnp.where(lane % PIECE == row, both[:, :LANES].reshape(lane.shape), 0.0)
    mean = jnp.sum(mean, axis=1, keepdims=True)
    x = y.astype(f32).reshape(lane.shape) + key_sum * mean
    x = jnp.where(lane < HEAD_DIM, x, jnp.where(lane == HEAD_DIM, key_sum, 0.0))
    return x.reshape(y.shape)


def encode_grad(x):
    lane = lax.broadcasted_iota(jnp.int32, x.shape, 1)
    low = pltpu.roll(x - x.astype(bf16).astype(f32), 1, 1)
    return jnp.where(lane == HEAD_DIM + 1, low, x).astype(WIRE)


def decode_grad(y):
    lane = lax.broadcasted_iota(jnp.int32, y.shape, 1)
    x = y.astype(f32)
    whole = x + pltpu.roll(x, LANES - 1, 1)
    return jnp.where(lane < HEAD_DIM, x, jnp.where(lane == HEAD_DIM, whole, 0.0))


def state_kernel(k_ref, v_ref, tot_ref, first_ref, send_ref):
    ks = [jnp.maximum(k_ref[rows_of(j), :], 0) for j in range(HALF)]
    vs = [with_one(v_ref[rows_of(j), :]) for j in range(HALF)]
    firsts = [dot(k[:, :FRAME], v[:, :FRAME], 1, 1) for k, v in zip(ks, vs)]
    seconds = [dot(k[:, FRAME:], v[:, FRAME:], 1, 1) for k, v in zip(ks, vs)]
    for j in range(HALF):
        tot = firsts[j] + seconds[j]
        first_ref[rows_of(j), :] = firsts[j]
        tot_ref[rows_of(j), :] = tot
        send_ref[rows_of(j), :] = encode(tot)


def scan_kernel(x_ref, o_ref):
    parts = [decode(x_ref[i]) for i in range(x_ref.shape[0])]
    totals = [jnp.zeros_like(parts[0])]
    for part in parts[:-1]:
        totals.append(totals[-1] + part)
    for i, total in enumerate([encode(total) for total in totals]):
        o_ref[i] = total


def scan_back_kernel(x_ref, conv_ref, o_ref):
    n, rows = x_ref.shape[:2]
    conv = conv_ref[...].astype(WIRE)
    parts = [decode_grad(x_ref[i]) for i in range(n)]
    totals = [jnp.zeros_like(parts[0])]
    for part in parts[:0:-1]:
        totals.append(totals[-1] + part)
    for i, total in enumerate([encode_grad(total) for total in totals]):
        o_ref[n - 1 - i, :rows] = total
        o_ref[n - 1 - i, rows:] = conv


def numerators(qs, states):
    nums = {u: dot(cat(states[u], 0), cat([qs[u]] * 2, 0), 0, 0) for u in qs}
    invs = {u: 1.0 / (num[HEAD_DIM : HEAD_DIM + 1] + denom_eps) for u, num in nums.items()}
    return {u: num[:HEAD_DIM] for u, num in nums.items()}, invs


def gradients(go, num, inv):
    gn = go * inv
    gden = -inv * jnp.sum(gn * num, axis=0, keepdims=True)
    return split(cat([gn, jnp.where(first_of_pad(FRAME), gden, 0.0)], 0))


def middle_kernel(
    q_ref, behind_ref, cot_ref, ahead_ref, w_ref, prev_ref, tot_ref, first_ref,
    att0_ref, att1_ref, att_behind_ref, gtot_ref, glast_ref, send_ref, conv_ref,
):
    step = pl.program_id(0)
    qs, states, cots, gos = {}, {}, {}, {}
    for j in range(HALF):
        rows = rows_of(j)
        q = jnp.maximum(q_ref[rows, :], 0)
        before = decode(prev_ref[rows, :])
        qs[j, -1] = jnp.maximum(behind_ref[rows, :], 0)
        states[j, -1] = split(before)
        for f in range(2):
            qs[j, f] = q[:, frames[f]]
            states[j, f] = split(before + (first_ref, tot_ref)[f][rows, :])
        w0, w1 = w_ref[rows, 0:1], w_ref[rows, 1:2]
        c0, c1 = parts_of(rows, cot_ref)
        c2 = ahead_ref[rows, :].astype(f32)
        cots[j] = c0, c1, c2
        gos[j, -1] = loss_scale * (w1 * c1)
        gos[j, 0] = loss_scale * (c0 + w0 * c1 + w1 * c2)
        gos[j, 1] = loss_scale * (c1 + w0 * c2)
    nums, invs = numerators(qs, states)
    atts = {u: (nums[u] * invs[u]).astype(bf16) for u in qs}
    grads = {u: gradients(gos[u], nums[u], invs[u]) for u in qs}
    gstates = {u: dot(cat([qs[u]] * 2, 1), cat(grads[u], 1), 1, 1) for u in qs}
    for j in range(HALF):
        rows = rows_of(j)
        own = gstates[j, 0] + gstates[j, 1]
        glast_ref[rows, :] = gstates[j, 1]
        gtot_ref[rows, :] = own
        send_ref[rows, :] = encode_grad(own + gstates[j, -1])
        att_behind_ref[rows, :], att0_ref[rows, :], att1_ref[rows, :] = (
            atts[j, f] for f in (-1, 0, 1)
        )
        wide = [atts[j, f].astype(f32) for f in (-1, 0)]
        c0, c1, c2 = cots[j]
        for i, part in enumerate([wide[0] * c0 + wide[1] * c1, wide[0] * c1 + wide[1] * c2]):
            line = jnp.sum(part.T, axis=0, keepdims=True)
            line = cat([line, jnp.zeros((1, LANES - HEAD_DIM), f32)], 1)
            conv_ref[pl.ds(i * HEADS + step * HALF + j, 1), :] = line

    @pl.when(step == 1)
    def _():
        conv_ref[2 * HEADS :, :] = jnp.zeros((TOLD - 2 * HEADS, LANES), f32)


def queries_kernel(
    q_ref, cot_ref, ahead_ref, ahead2_ref, w_ref, prev_ref, tot_ref, first_ref, gq_ref
):
    qs, states, gos = {}, {}, {}
    for j in range(HALF):
        rows = rows_of(j)
        q = jnp.maximum(q_ref[rows, :], 0)
        before = decode(prev_ref[rows, :])
        c = parts_of(rows, cot_ref) + [r[rows, :].astype(f32) for r in (ahead_ref, ahead2_ref)]
        for f in range(2):
            qs[j, f] = q[:, frames[f]]
            states[j, f] = split(before + (first_ref, tot_ref)[f][rows, :])
            gos[j, f] = loss_scale * filtered(c[f : f + 3], w_ref, rows)
    nums, invs = numerators(qs, states)
    for j, f in qs:
        u = j, f
        (hi, lo), (ghi, glo) = states[u], gradients(gos[u], nums[u], invs[u])
        gq = dot(cat([hi, hi, lo], 1), cat([ghi, glo, ghi], 0), 1, 0)
        gq = jnp.where(qs[u].astype(f32) > 0, gq, 0.0)
        gq_ref[rows_of(j), frames[f]] = gq.astype(bf16)


def mixed_kernel(att0_ref, att1_ref, behind_ref, behind2_ref, w_ref, mix_ref):
    for j in range(HALF):
        rows = rows_of(j)
        c = [r[rows, :].astype(f32) for r in (behind2_ref, behind_ref, att0_ref, att1_ref)]
        for f in range(2):
            mix_ref[rows, frames[f]] = filtered(c[f : f + 3][::-1], w_ref, rows).astype(bf16)


def last_kernel(chunk, k_ref, v_ref, follow_ref, gtot_ref, glast_ref, gk_ref, gv_ref, conv_ref):
    stride = chunk + TOLD
    starts = range(0, follow_ref.shape[0], stride)
    conv = sum(follow_ref[i + chunk : i + stride, :].astype(f32) for i in starts)

    @pl.when(pl.program_id(0) == 0)
    def _():
        conv_ref[...] = conv

    @pl.when(pl.program_id(0) > 0)
    def _():
        conv_ref[...] += conv

    ks, vs, states = {}, {}, {}
    for j in range(HALF):
        rows = rows_of(j)
        k = jnp.maximum(k_ref[rows, :], 0)
        v = with_one(v_ref[rows, :])
        pieces = []
        for at in range(rows.start, rows.stop, PIECE):
            place = at // chunk * stride + at % chunk
            pieces.append(follow_ref[place : place + PIECE, :])
        behind = decode_grad(cat(pieces, 0))
        for f in range(2):
            ks[j, f], vs[j, f] = k[:, frames[f]], v[:, frames[f]]
            states[j, f] = split(behind + (gtot_ref, glast_ref)[f][rows, :])
    gvs = {u: dot(cat(states[u], 0), cat([ks[u]] * 2, 0), 0, 0) for u in units}
    gks = {u: dot(cat(states[u], 1), cat([vs[u]] * 2, 0), 1, 0) for u in units}
    for j, f in units:
        rows = rows_of(j)
        gv_ref[rows, frames[f]] = gvs[j, f][:HEAD_DIM].astype(bf16)
        gk = jnp.where(ks[j, f].astype(f32) > 0, gks[j, f], 0.0)
        gk_ref[rows, frames[f]] = gk.astype(bf16)


def call(kernel, name, outs, *args, whole=()):
    def spec(x):
        if any(x is w for w in whole):
            return pl.BlockSpec(x.shape, lambda g: (0, 0))
        return pl.BlockSpec((x.shape[0] // 2, x.shape[1]), lambda g: (g, 0))

    return pl.pallas_call(
        kernel,
        grid=(2,),
        in_specs=[spec(a) for a in args],
        out_specs=[spec(o) for o in outs],
        out_shape=outs,
        compiler_params=PARAMS,
        name=name,
    )(*args)


def scan(kernel, name, x, told=None):
    n, rows = x.shape[:2]
    args = (x,) if told is None else (x, told)
    return pl.pallas_call(
        kernel,
        out_shape=shape(n, rows + sum(a.shape[0] for a in args[1:]), LANES, dtype=WIRE),
        compiler_params=PARAMS,
        name=name,
    )(*args)


def exchange(x, axis):
    return lax.all_to_all(x, axis, 0, 0, tiled=True)


def from_behind(block, axis, distance):
    devices = range(lax.axis_size(axis))
    route = [(i - distance, i) for i in devices if i - distance in devices]
    return lax.ppermute(block, axis, route)


def total_over(x, axis):
    n = lax.axis_size(axis)
    bit = 1
    while bit < n:
        masks = [bit] if 2 * bit == n else [bit, 2 * bit, 3 * bit]
        x = x + sum(lax.ppermute(x, axis, [(i, i ^ m) for i in range(n)]) for m in masks)
        bit *= 4
    return x


def body(queries, keys, values, cotangent, conv_weight):
    clips, toks, width = queries.shape
    q, k, v, cot = (x.reshape(toks, width).T for x in (queries, keys, values, cotangent))
    weight = conv_weight.T
    n = lax.axis_size("seq")
    chunk = -(-HALF_ROWS // (PIECE * (n // 2))) * PIECE
    state = shape(chunk * n, LANES)
    sent = shape(*state.shape, dtype=WIRE)
    tokens = shape(width, toks, dtype=bf16)

    half_tokens = shape(width, FRAME, dtype=bf16)

    behind = from_behind(q[:, FRAME:], "seq", 1)
    ahead = from_behind(cot[:, :FRAME], "seq", -1)
    tot, first, send = call(state_kernel, "states", [state, state, sent], k, v)
    got = exchange(send.reshape(n, chunk, LANES), "seq")
    prev = exchange(scan(scan_kernel, "scan", got), "seq").reshape(state.shape)
    ahead2, prev = lax.optimization_barrier((cot[:, FRAME:], prev))
    ahead2 = from_behind(ahead2, "seq", -1)
    conv = shape(TOLD, LANES)
    att0, att1, att_behind, gtot, glast, send, conv = call(
        middle_kernel, "middle",
        [half_tokens, half_tokens, half_tokens, state, state, sent, conv],
        q, behind, cot, ahead, weight, prev, tot, first, whole=[conv],
    )
    conv = total_over(conv, "dp")
    got = exchange(send.reshape(n, chunk, LANES), "seq")
    att_behind2 = from_behind(att0, "seq", 1)
    follow = scan(scan_back_kernel, "scan_back", got, conv)
    att_behind2 = lax.optimization_barrier((att_behind2, follow))[0]
    ahead2 = lax.optimization_barrier((ahead2, follow))[0]
    follow, att_behind2, ahead2 = lax.optimization_barrier((follow, att_behind2, ahead2))
    follow = exchange(follow, "seq").reshape(-1, LANES)
    (gq,) = call(
        queries_kernel, "queries", [tokens], q, cot, ahead, ahead2, weight, prev, tot, first
    )
    (mixed,) = call(
        mixed_kernel, "mixed", [tokens], att0, att1, att_behind, att_behind2, weight
    )
    conv = shape(TOLD, LANES)
    gk, gv, conv = call(
        functools.partial(last_kernel, chunk), "last", [tokens, tokens, conv],
        k, v, follow, gtot, glast, whole=[conv],
    )
    conv = conv[: 2 * HEADS].reshape(2, HEADS, LANES)[:, :, :HEAD_DIM].reshape(2, width)
    conv = conv / (clips * lax.axis_size("dp"))
    return tuple(x.T.reshape(clips, toks, width) for x in (mixed, gq, gk, gv)) + (conv,)


def solution(mesh):
    blocks = P("dp", "seq", None)
    return jax.shard_map(
        body,
        mesh=mesh,
        in_specs=(blocks,) * 4 + (P(),),
        out_specs=(blocks,) * 4 + (P(),),
        check_vma=False,
    )
```

```python
import functools

import jax
import jax.numpy as jnp
from jax import lax
from jax.experimental import pallas as pl
from jax.experimental.pallas import tpu as pltpu
from jax.sharding import PartitionSpec as P

HEADS = 20
HEAD_DIM = 112
FRAME = 128
LANES = 128
HALF = HEADS // 2
HALF_ROWS = HALF * HEAD_DIM
PIECE = 16
TOLD = 48
WIRE = jnp.bfloat16

denom_eps = 1e-06
loss_scale = 16.0
f32 = jnp.float32
bf16 = jnp.bfloat16

PARAMS = pltpu.CompilerParams(vmem_limit_bytes=56 * 2**20)
frames = [slice(0, FRAME), slice(FRAME, 2 * FRAME)]
units = [(j, f) for j in range(HALF) for f in range(2)]


def shape(*dims, dtype=f32):
    return jax.ShapeDtypeStruct(dims, dtype)


def split(x):
    high = x.astype(bf16)
    return high, (x - high.astype(f32)).astype(bf16)


def dot(a, b, ca, cb):
    return lax.dot_general(a, b, (((ca,), (cb,)), ((), ())), preferred_element_type=f32)


def cat(parts, axis):
    return jnp.concatenate(parts, axis=axis)


def first_of_pad(columns):
    return lax.broadcasted_iota(jnp.int32, (LANES - HEAD_DIM, columns), 0) == 0


def with_one(v):
    return cat([v, jnp.where(first_of_pad(v.shape[1]), 1.0, 0.0).astype(bf16)], 0)


def rows_of(j):
    return slice(j * HEAD_DIM, (j + 1) * HEAD_DIM)


def filtered(c, w_ref, rows):
    w0, w1 = w_ref[rows, 0:1], w_ref[rows, 1:2]
    return c[0] + w0 * c[1] + w1 * c[2]


def parts_of(rows, *refs):
    return [ref[rows, fr].astype(f32) for ref in refs for fr in frames]


def grid_of(rows):
    dims = (rows // PIECE, PIECE, LANES)
    return [lax.broadcasted_iota(jnp.int32, dims, d) for d in (2, 1)]


def slots():
    channel = lax.broadcasted_iota(jnp.int32, (LANES, LANES), 0)
    column = lax.broadcasted_iota(jnp.int32, (LANES, LANES), 1)
    hit = (channel < HEAD_DIM) & (column - (HEAD_DIM + 2) == channel // PIECE)
    return jnp.where(hit, 1.0, 0.0).astype(bf16)


def encode(x):
    lane, row = grid_of(x.shape[0])
    x3 = x.reshape(lane.shape)
    sums = jnp.sum(x3, axis=1, keepdims=True)
    mean = sums / (sums[:, :, HEAD_DIM : HEAD_DIM + 1] + 1e-30)
    mean = jnp.where(lane[:, :1] < HEAD_DIM, mean, 0.0).astype(bf16).astype(f32)
    key_sum = x3[:, :, HEAD_DIM : HEAD_DIM + 1]
    low = key_sum - key_sum.astype(bf16).astype(f32)
    y = jnp.where(lane == HEAD_DIM + 1, low, x3 - key_sum * mean)
    kept = jnp.where(lane % PIECE == row, mean, 0.0).reshape(x.shape).astype(bf16)
    return (y.reshape(x.shape) + dot(kept, slots(), 1, 0)).astype(WIRE)


def decode(y):
    lane, row = grid_of(y.shape[0])
    column = lax.broadcasted_iota(jnp.int32, (LANES, LANES), 1)
    pair = (column == HEAD_DIM) | (column == HEAD_DIM + 1)
    pair = jnp.where(pair, 1.0, 0.0).astype(bf16)
    both = dot(y, cat([slots(), pair], 0), 1, 1)
    key_sum = both[:, LANES:].reshape(lane.shape)
    mean = jnp.where(lane % PIECE == row, both[:, :LANES].reshape(lane.shape), 0.0)
    mean = jnp.sum(mean, axis=1, keepdims=True)
    x = y.astype(f32).reshape(lane.shape) + key_sum * mean
    x = jnp.where(lane < HEAD_DIM, x, jnp.where(lane == HEAD_DIM, key_sum, 0.0))
    return x.reshape(y.shape)


def encode_grad(x):
    lane = lax.broadcasted_iota(jnp.int32, x.shape, 1)
    low = pltpu.roll(x - x.astype(bf16).astype(f32), 1, 1)
    return jnp.where(lane == HEAD_DIM + 1, low, x).astype(WIRE)


def decode_grad(y):
    lane = lax.broadcasted_iota(jnp.int32, y.shape, 1)
    x = y.astype(f32)
    whole = x + pltpu.roll(x, LANES - 1, 1)
    return jnp.where(lane < HEAD_DIM, x, jnp.where(lane == HEAD_DIM, whole, 0.0))


def state_kernel(k_ref, v_ref, tot_ref, first_ref, send_ref):
    ks = [jnp.maximum(k_ref[rows_of(j), :], 0) for j in range(HALF)]
    vs = [with_one(v_ref[rows_of(j), :]) for j in range(HALF)]
    firsts = [dot(k[:, :FRAME], v[:, :FRAME], 1, 1) for k, v in zip(ks, vs)]
    seconds = [dot(k[:, FRAME:], v[:, FRAME:], 1, 1) for k, v in zip(ks, vs)]
    for j in range(HALF):
        tot = firsts[j] + seconds[j]
        first_ref[rows_of(j), :] = firsts[j]
        tot_ref[rows_of(j), :] = tot
        send_ref[rows_of(j), :] = encode(tot)


def scan_kernel(x_ref, o_ref):
    parts = [decode(x_ref[i]) for i in range(x_ref.shape[0])]
    totals = [jnp.zeros_like(parts[0])]
    for part in parts[:-1]:
        totals.append(totals[-1] + part)
    for i, total in enumerate([encode(total) for total in totals]):
        o_ref[i] = total


def scan_back_kernel(x_ref, conv_ref, o_ref):
    n, rows = x_ref.shape[:2]
    conv = conv_ref[...].astype(WIRE)
    parts = [decode_grad(x_ref[i]) for i in range(n)]
    totals = [jnp.zeros_like(parts[0])]
    for part in parts[:0:-1]:
        totals.append(totals[-1] + part)
    for i, total in enumerate([encode_grad(total) for total in totals]):
        o_ref[n - 1 - i, :rows] = total
        o_ref[n - 1 - i, rows:] = conv


def numerators(qs, states):
    nums = {u: dot(cat(states[u], 0), cat([qs[u]] * 2, 0), 0, 0) for u in qs}
    invs = {u: 1.0 / (num[HEAD_DIM : HEAD_DIM + 1] + denom_eps) for u, num in nums.items()}
    return {u: num[:HEAD_DIM] for u, num in nums.items()}, invs


def gradients(go, num, inv):
    gn = go * inv
    gden = -inv * jnp.sum(gn * num, axis=0, keepdims=True)
    return split(cat([gn, jnp.where(first_of_pad(FRAME), gden, 0.0)], 0))


def middle_kernel(
    q_ref, behind_ref, cot_ref, ahead_ref, w_ref, prev_ref, tot_ref, first_ref,
    att0_ref, att1_ref, att_behind_ref, gtot_ref, glast_ref, send_ref, conv_ref,
):
    step = pl.program_id(0)
    qs, states, cots, gos = {}, {}, {}, {}
    for j in range(HALF):
        rows = rows_of(j)
        q = jnp.maximum(q_ref[rows, :], 0)
        before = decode(prev_ref[rows, :])
        qs[j, -1] = jnp.maximum(behind_ref[rows, :], 0)
        states[j, -1] = split(before)
        for f in range(2):
            qs[j, f] = q[:, frames[f]]
            states[j, f] = split(before + (first_ref, tot_ref)[f][rows, :])
        w0, w1 = w_ref[rows, 0:1], w_ref[rows, 1:2]
        c0, c1 = parts_of(rows, cot_ref)
        c2 = ahead_ref[rows, :].astype(f32)
        cots[j] = c0, c1, c2
        gos[j, -1] = loss_scale * (w1 * c1)
        gos[j, 0] = loss_scale * (c0 + w0 * c1 + w1 * c2)
        gos[j, 1] = loss_scale * (c1 + w0 * c2)
    nums, invs = numerators(qs, states)
    atts = {u: (nums[u] * invs[u]).astype(bf16) for u in qs}
    grads = {u: gradients(gos[u], nums[u], invs[u]) for u in qs}
    gstates = {u: dot(cat([qs[u]] * 2, 1), cat(grads[u], 1), 1, 1) for u in qs}
    for j in range(HALF):
        rows = rows_of(j)
        own = gstates[j, 0] + gstates[j, 1]
        glast_ref[rows, :] = gstates[j, 1]
        gtot_ref[rows, :] = own
        send_ref[rows, :] = encode_grad(own + gstates[j, -1])
        att_behind_ref[rows, :], att0_ref[rows, :], att1_ref[rows, :] = (
            atts[j, f] for f in (-1, 0, 1)
        )
        wide = [atts[j, f].astype(f32) for f in (-1, 0)]
        c0, c1, c2 = cots[j]
        for i, part in enumerate([wide[0] * c0 + wide[1] * c1, wide[0] * c1 + wide[1] * c2]):
            line = jnp.sum(part.T, axis=0, keepdims=True)
            line = cat([line, jnp.zeros((1, LANES - HEAD_DIM), f32)], 1)
            conv_ref[pl.ds(i * HEADS + step * HALF + j, 1), :] = line

    @pl.when(step == 1)
    def _():
        conv_ref[2 * HEADS :, :] = jnp.zeros((TOLD - 2 * HEADS, LANES), f32)


def queries_kernel(
    q_ref, cot_ref, ahead_ref, ahead2_ref, w_ref, prev_ref, tot_ref, first_ref, gq_ref
):
    qs, states, gos = {}, {}, {}
    for j in range(HALF):
        rows = rows_of(j)
        q = jnp.maximum(q_ref[rows, :], 0)
        before = decode(prev_ref[rows, :])
        c = parts_of(rows, cot_ref) + [r[rows, :].astype(f32) for r in (ahead_ref, ahead2_ref)]
        for f in range(2):
            qs[j, f] = q[:, frames[f]]
            states[j, f] = split(before + (first_ref, tot_ref)[f][rows, :])
            gos[j, f] = loss_scale * filtered(c[f : f + 3], w_ref, rows)
    nums, invs = numerators(qs, states)
    for j, f in qs:
        u = j, f
        (hi, lo), (ghi, glo) = states[u], gradients(gos[u], nums[u], invs[u])
        gq = dot(cat([hi, hi, lo], 1), cat([ghi, glo, ghi], 0), 1, 0)
        gq = jnp.where(qs[u].astype(f32) > 0, gq, 0.0)
        gq_ref[rows_of(j), frames[f]] = gq.astype(bf16)


def mixed_kernel(att0_ref, att1_ref, behind_ref, behind2_ref, w_ref, mix_ref):
    for j in range(HALF):
        rows = rows_of(j)
        c = [r[rows, :].astype(f32) for r in (behind2_ref, behind_ref, att0_ref, att1_ref)]
        for f in range(2):
            mix_ref[rows, frames[f]] = filtered(c[f : f + 3][::-1], w_ref, rows).astype(bf16)


def last_kernel(chunk, k_ref, v_ref, follow_ref, gtot_ref, glast_ref, gk_ref, gv_ref, conv_ref):
    stride = chunk + TOLD
    starts = range(0, follow_ref.shape[0], stride)
    conv = sum(follow_ref[i + chunk : i + stride, :].astype(f32) for i in starts)

    @pl.when(pl.program_id(0) == 0)
    def _():
        conv_ref[...] = conv

    @pl.when(pl.program_id(0) > 0)
    def _():
        conv_ref[...] += conv

    ks, vs, states = {}, {}, {}
    for j in range(HALF):
        rows = rows_of(j)
        k = jnp.maximum(k_ref[rows, :], 0)
        v = with_one(v_ref[rows, :])
        pieces = []
        for at in range(rows.start, rows.stop, PIECE):
            place = at // chunk * stride + at % chunk
            pieces.append(follow_ref[place : place + PIECE, :])
        behind = decode_grad(cat(pieces, 0))
        for f in range(2):
            ks[j, f], vs[j, f] = k[:, frames[f]], v[:, frames[f]]
            states[j, f] = split(behind + (gtot_ref, glast_ref)[f][rows, :])
    gvs = {u: dot(cat(states[u], 0), cat([ks[u]] * 2, 0), 0, 0) for u in units}
    gks = {u: dot(cat(states[u], 1), cat([vs[u]] * 2, 0), 1, 0) for u in units}
    for j, f in units:
        rows = rows_of(j)
        gv_ref[rows, frames[f]] = gvs[j, f][:HEAD_DIM].astype(bf16)
        gk = jnp.where(ks[j, f].astype(f32) > 0, gks[j, f], 0.0)
        gk_ref[rows, frames[f]] = gk.astype(bf16)


def call(kernel, name, outs, *args, whole=()):
    def spec(x):
        if any(x is w for w in whole):
            return pl.BlockSpec(x.shape, lambda g: (0, 0))
        return pl.BlockSpec((x.shape[0] // 2, x.shape[1]), lambda g: (g, 0))

    return pl.pallas_call(
        kernel,
        grid=(2,),
        in_specs=[spec(a) for a in args],
        out_specs=[spec(o) for o in outs],
        out_shape=outs,
        compiler_params=PARAMS,
        name=name,
    )(*args)


def scan(kernel, name, x, told=None):
    n, rows = x.shape[:2]
    args = (x,) if told is None else (x, told)
    return pl.pallas_call(
        kernel,
        out_shape=shape(n, rows + sum(a.shape[0] for a in args[1:]), LANES, dtype=WIRE),
        compiler_params=PARAMS,
        name=name,
    )(*args)


def exchange(x, axis):
    return lax.all_to_all(x, axis, 0, 0, tiled=True)


def from_behind(block, axis, distance):
    devices = range(lax.axis_size(axis))
    route = [(i - distance, i) for i in devices if i - distance in devices]
    return lax.ppermute(block, axis, route)


def total_over(x, axis, bit):
    n = lax.axis_size(axis)
    masks = [m for m in (bit, 2 * bit, 3 * bit) if m < n]
    return x + sum(lax.ppermute(x, axis, [(i, i ^ m) for i in range(n)]) for m in masks)


def body(queries, keys, values, cotangent, conv_weight):
    clips, toks, width = queries.shape
    q, k, v, cot = (x.reshape(toks, width).T for x in (queries, keys, values, cotangent))
    weight = conv_weight.T
    n = lax.axis_size("seq")
    chunk = -(-HALF_ROWS // (PIECE * (n // 2))) * PIECE
    state = shape(chunk * n, LANES)
    sent = shape(*state.shape, dtype=WIRE)
    tokens = shape(width, toks, dtype=bf16)

    half_tokens = shape(width, FRAME, dtype=bf16)

    behind = from_behind(q[:, FRAME:], "seq", 1)
    ahead = from_behind(cot[:, :FRAME], "seq", -1)
    tot, first, send = call(state_kernel, "states", [state, state, sent], k, v)
    got = exchange(send.reshape(n, chunk, LANES), "seq")
    prev = exchange(scan(scan_kernel, "scan", got), "seq").reshape(state.shape)
    ahead2, prev = lax.optimization_barrier((cot[:, FRAME:], prev))
    ahead2 = from_behind(ahead2, "seq", -1)
    conv = shape(TOLD, LANES)
    att0, att1, att_behind, gtot, glast, send, conv = call(
        middle_kernel, "middle",
        [half_tokens, half_tokens, half_tokens, state, state, sent, conv],
        q, behind, cot, ahead, weight, prev, tot, first, whole=[conv],
    )
    conv = total_over(conv, "dp", 1)
    got = exchange(send.reshape(n, chunk, LANES), "seq")
    att_behind2 = from_behind(att0, "seq", 1)
    follow = scan(scan_back_kernel, "scan_back", got, conv)
    att_behind2 = lax.optimization_barrier((att_behind2, follow))[0]
    ahead2 = lax.optimization_barrier((ahead2, follow))[0]
    follow, att_behind2, ahead2 = lax.optimization_barrier((follow, att_behind2, ahead2))
    follow = exchange(follow, "seq").reshape(-1, LANES)
    (gq,) = call(
        queries_kernel, "queries", [tokens], q, cot, ahead, ahead2, weight, prev, tot, first
    )
    (mixed,) = call(
        mixed_kernel, "mixed", [tokens], att0, att1, att_behind, att_behind2, weight
    )
    follow, gq, mixed = lax.optimization_barrier((follow, gq, mixed))
    conv = shape(TOLD, LANES)
    gk, gv, conv = call(
        functools.partial(last_kernel, chunk), "last", [tokens, tokens, conv],
        k, v, follow, gtot, glast, whole=[conv],
    )
    conv = total_over(conv[: 2 * HEADS], "dp", 4)
    conv = conv.reshape(2, HEADS, LANES)[:, :, :HEAD_DIM].reshape(2, width)
    conv = conv / (clips * lax.axis_size("dp"))
    return tuple(x.T.reshape(clips, toks, width) for x in (mixed, gq, gk, gv)) + (conv,)


def solution(mesh):
    blocks = P("dp", "seq", None)
    return jax.shard_map(
        body,
        mesh=mesh,
        in_specs=(blocks,) * 4 + (P(),),
        out_specs=(blocks,) * 4 + (P(),),
        check_vma=False,
    )
```
